32 devices in a mesh: row: 8 (over y, x, core), col: 4 (over z).
Axes of the slice: x: 2, y: 2, z: 4, core: 2. Of those that a mesh axis runs over, the one named last changes fastest.
Arguments:
- radar_tiles: bfloat16 [512, 256, 256], P('row', 'col'), may hold values from -6 to 6
- conv_scale: float32 [256], replicated, may hold values from 0.5 to 1.5
- conv_shift: float32 [256], replicated, may hold values from -3 to 3
- expand_weight: bfloat16 [256, 1024], replicated, may hold values from -0.375 to 0.375
- expand_bias: float32 [1024], replicated, may hold values from -3 to 3
- depth_kernel: float32 [3, 3, 1024], replicated, may hold values from -2 to 2
- depth_bias: float32 [1024], replicated, may hold values from -3 to 3
- project_weight: bfloat16 [1024, 256], replicated, may hold values from -0.1875 to 0.1875
- block_gains: float32 [2, 256], replicated, may hold values from 0.5 to 1.5
- block_entry: bfloat16 [256, 768], replicated, may hold values from -0.375 to 0.375
- block_leave: bfloat16 [256, 256], replicated, may hold values from -0.375 to 0.375
- block_offsets: float32 [8, 64, 64], replicated, may hold values from -6 to 6
- block_widen: bfloat16 [256, 1024], replicated, may hold values from -0.375 to 0.375
- block_shrink: bfloat16 [1024, 256], replicated, may hold values from -0.1875 to 0.1875
- grid_gains: float32 [2, 256], replicated, may hold values from 0.5 to 1.5
- grid_entry: bfloat16 [256, 768], replicated, may hold values from -0.375 to 0.375
- grid_leave: bfloat16 [256, 256], replicated, may hold values from -0.375 to 0.375
- grid_offsets: float32 [8, 64, 64], replicated, may hold values from -6 to 6
- grid_widen: bfloat16 [256, 1024], replicated, may hold values from -0.375 to 0.375
- grid_shrink: bfloat16 [1024, 256], replicated, may hold values from -0.1875 to 0.1875
Outputs:
- refined: bfloat16 [512, 256, 256], P('row', 'col')
The draws below stay inside these ranges and needn't reach their ends.
All inputs are finite; a program needn't handle non-finite values.
Results may differ from the reference program's by a relative error of at most 0.015.
Values may be sent and summed in bfloat16 or wider, within the bound.
A program may use at most 128 MiB of HBM per device.

```python
import math
import jax
import jax.numpy as jnp
from jax import lax

D = 256
HEADS = 8
WIN = 8
INNER = 1024
HEIGHT = 512
BREADTH = 256
N_ROW = 8
N_COL = 4


def level_of(rng, extent, shards, low, top_value):
    def one(dim, shards_of):
        steps = jax.random.uniform(jax.random.fold_in(jax.random.fold_in(rng, 6), dim), (shards_of,), jnp.float32, low / len(shards), top_value / len(shards))
        return jnp.repeat(jnp.exp(steps), extent[dim] // shards_of).reshape((-1,) + (1,) * (len(extent) - dim - 1))

    level = one(*shards[0])
    for cut in shards[1:]:
        level = level * one(*cut)
    return level


def noise(stream_key, dims, deviation, bound, pieces=(), kind=jnp.bfloat16):
    values = deviation * jax.random.normal(stream_key, dims, jnp.float32)
    if pieces:
        values = values * level_of(stream_key, dims, pieces, -0.22, 0.18)
    return jnp.clip(values, -bound, bound).astype(kind)


def setup_inputs(seed: int = 0) -> dict:
    key_of = jax.random.split(jax.random.key(seed), 21)
    radar_tiles = noise(key_of[0], (HEIGHT, BREADTH, D), 1.0, 6.0, ((0, 8), (1, 4)))
    conv_scale = jnp.clip(jax.random.uniform(key_of[1], (D,), jnp.float32, 0.5, 1.5), 0.5, 1.5)
    conv_shift = noise(key_of[2], (D,), 0.5, 3.0, (), jnp.float32)
    expand_weight = noise(key_of[3], (D, INNER), D ** -0.5, 0.375)
    expand_bias = noise(key_of[4], (INNER,), 0.5, 3.0, (), jnp.float32)
    depth_kernel = noise(key_of[5], (3, 3, INNER), 9 ** -0.5, 2.0, (), jnp.float32)
    depth_bias = noise(key_of[6], (INNER,), 0.5, 3.0, (), jnp.float32)
    project_weight = noise(key_of[7], (INNER, D), INNER ** -0.5, 0.1875)
    block_gains = jnp.clip(jax.random.uniform(key_of[8], (2, D), jnp.float32, 0.5, 1.5), 0.5, 1.5)
    block_entry = noise(key_of[9], (D, 3 * D), D ** -0.5, 0.375)
    block_leave = noise(key_of[10], (D, D), D ** -0.5, 0.375)
    block_offsets = noise(key_of[11], (HEADS, WIN * WIN, WIN * WIN), 1.0, 6.0, (), jnp.float32)
    block_widen = noise(key_of[12], (D, INNER), D ** -0.5, 0.375)
    block_shrink = noise(key_of[13], (INNER, D), INNER ** -0.5, 0.1875)
    grid_gains = jnp.clip(jax.random.uniform(key_of[14], (2, D), jnp.float32, 0.5, 1.5), 0.5, 1.5)
    grid_entry = noise(key_of[15], (D, 3 * D), D ** -0.5, 0.375)
    grid_leave = noise(key_of[16], (D, D), D ** -0.5, 0.375)
    grid_offsets = noise(key_of[17], (HEADS, WIN * WIN, WIN * WIN), 1.0, 6.0, (), jnp.float32)
    grid_widen = noise(key_of[18], (D, INNER), D ** -0.5, 0.375)
    grid_shrink = noise(key_of[19], (INNER, D), INNER ** -0.5, 0.1875)
    return {"radar_tiles": radar_tiles, "conv_scale": conv_scale, "conv_shift": conv_shift, "expand_weight": expand_weight, "expand_bias": expand_bias, "depth_kernel": depth_kernel, "depth_bias": depth_bias, "project_weight": project_weight, "block_gains": block_gains, "block_entry": block_entry, "block_leave": block_leave, "block_offsets": block_offsets, "block_widen": block_widen, "block_shrink": block_shrink, "grid_gains": grid_gains, "grid_entry": grid_entry, "grid_leave": grid_leave, "grid_offsets": grid_offsets, "grid_widen": grid_widen, "grid_shrink": grid_shrink}


epsilon = 1e-05

def layer_norm(values, gain_row):
    center = values - lax.optimization_barrier(jnp.mean(values, axis=-1, keepdims=True))
    spread = lax.optimization_barrier(jnp.mean(center * center, axis=-1, keepdims=True))
    return center * lax.rsqrt(spread + epsilon) * gain_row

def attend(windows, norm_gains, entry_weight, leave_weight, offset_table, widen_weight, shrink_weight):
    win_count, positions, channels = windows.shape
    head_count = offset_table.shape[0]
    head_size = channels // head_count
    flattened = windows.reshape(-1, channels).astype(jnp.float32)
    lifted = layer_norm(flattened, norm_gains[0]).astype(jnp.bfloat16)
    projected = jnp.dot(lifted, entry_weight, preferred_element_type=jnp.float32).astype(jnp.bfloat16)
    projected = projected.reshape(win_count, positions, 3, head_count, head_size).astype(jnp.float32)
    query_rows = projected[:, :, 0]
    key_rows = projected[:, :, 1]
    value_rows = projected[:, :, 2]
    score_scale = 1.0 / math.sqrt(head_size)
    scores = jnp.einsum('nqhd,nkhd->nhqk', query_rows, key_rows) * score_scale + offset_table
    weights = jnp.exp(scores)
    weights = (weights / lax.optimization_barrier(jnp.sum(weights, axis=-1, keepdims=True))).astype(jnp.bfloat16)
    mixture = jnp.einsum('nhqk,nkhd->nqhd', weights.astype(jnp.float32), value_rows)
    mixture = mixture.astype(jnp.bfloat16).reshape(-1, channels)
    attended = (flattened + jnp.dot(mixture, leave_weight, preferred_element_type=jnp.float32)).astype(jnp.bfloat16)
    second = layer_norm(attended.astype(jnp.float32), norm_gains[1]).astype(jnp.bfloat16)
    hidden = jax.nn.gelu(jnp.dot(second, widen_weight, preferred_element_type=jnp.float32)).astype(jnp.bfloat16)
    result = attended.astype(jnp.float32) + jnp.dot(hidden, shrink_weight, preferred_element_type=jnp.float32)
    return result.astype(jnp.bfloat16).reshape(win_count, positions, channels)

def reference(radar_tiles, conv_scale, conv_shift, expand_weight, expand_bias, depth_kernel, depth_bias, project_weight, block_gains, block_entry, block_leave, block_offsets, block_widen, block_shrink, grid_gains, grid_entry, grid_leave, grid_offsets, grid_widen, grid_shrink):
    source = radar_tiles.astype(jnp.float32)
    normed = (source * conv_scale + conv_shift).astype(jnp.bfloat16)
    padded = jnp.pad(normed, ((1, 1), (1, 1), (0, 0)))
    inside = jnp.pad(jnp.ones((HEIGHT, BREADTH, 1), jnp.float32), ((1, 1), (1, 1), (0, 0)))

    def strip_work(strip_index):
        first_row = strip_index * WIN
        window_in = lax.dynamic_slice_in_dim(padded, first_row, WIN + 2, 0)
        window_mask = lax.dynamic_slice_in_dim(inside, first_row, WIN + 2, 0)
        lifted = jax.nn.gelu(jnp.dot(window_in.reshape(-1, D), expand_weight, preferred_element_type=jnp.float32) + expand_bias).astype(jnp.bfloat16)
        lifted = lifted.reshape(WIN + 2, BREADTH + 2, INNER) * window_mask.astype(jnp.bfloat16)
        summed = jnp.zeros((WIN, BREADTH, INNER), jnp.float32)
        for shift_row in range(3):
            for shift_col in range(3):
                summed = summed + lifted[shift_row:shift_row + WIN, shift_col:shift_col + BREADTH].astype(jnp.float32) * depth_kernel[shift_row, shift_col]
        activated = jax.nn.gelu(summed + depth_bias).astype(jnp.bfloat16)
        rows_in = lax.dynamic_slice_in_dim(source, first_row, WIN, 0)
        product = jnp.dot(activated.reshape(-1, INNER), project_weight, preferred_element_type=jnp.float32)
        return (rows_in + product.reshape(WIN, BREADTH, D)).astype(jnp.bfloat16)
    section_one = lax.map(strip_work, jnp.arange(HEIGHT // WIN, dtype=jnp.int32)).reshape(HEIGHT, BREADTH, D)
    blocks = section_one.reshape(HEIGHT // WIN, WIN, BREADTH // WIN, WIN, D).transpose(0, 2, 1, 3, 4)
    blocks = blocks.reshape(N_ROW * N_COL, -1, WIN * WIN, D)

    def block_work(window_group):
        return attend(window_group, block_gains, block_entry, block_leave, block_offsets, block_widen, block_shrink)
    attended_tiles = lax.map(block_work, blocks)
    section_two = attended_tiles.reshape(HEIGHT // WIN, BREADTH // WIN, WIN, WIN, D).transpose(0, 2, 1, 3, 4)
    section_two = section_two.reshape(HEIGHT, BREADTH, D)
    grid_sets = section_two.reshape(WIN, HEIGHT // WIN, WIN, BREADTH // WIN, D).transpose(1, 3, 0, 2, 4)
    grid_sets = grid_sets.reshape(N_ROW * N_COL, -1, WIN * WIN, D)

    def grid_work(window_group):
        return attend(window_group, grid_gains, grid_entry, grid_leave, grid_offsets, grid_widen, grid_shrink)
    spread = lax.map(grid_work, grid_sets)
    refined = spread.reshape(HEIGHT // WIN, BREADTH // WIN, WIN, WIN, D).transpose(2, 0, 3, 1, 4)
    return refined.reshape(HEIGHT, BREADTH, D)
```

```python
import functools
import math

import jax
import jax.numpy as jnp
from jax import lax
from jax.experimental import pallas as pl
from jax.experimental.pallas import tpu as pltpu
from jax.sharding import PartitionSpec as P

WIN = 8
LAG = 2
LANES = 128
MESH = pl.DeviceIdType.MESH

epsilon = 1e-05
f32 = jnp.float32
bf16 = jnp.bfloat16


def gelu(v):
    c = math.sqrt(2.0 / math.pi)
    return v * (0.5 + 0.5 * jnp.tanh(v * (c + (c * 0.044715) * (v * v))))


def dot(a, b):
    return jnp.dot(a, b, preferred_element_type=f32)


def dot_t(a, b):
    return lax.dot_general(a, b, (((1,), (1,)), ((), ())), preferred_element_type=f32)


def layer_norm(values, gain_row):
    center = values - jnp.mean(values, axis=-1, keepdims=True)
    spread = jnp.mean(center * center, axis=-1, keepdims=True)
    return (center * lax.rsqrt(spread + epsilon) * gain_row).astype(bf16)


def attend(x, heads, gains, entry, leave, offsets, widen, shrink, mask, ones, exps, mixed):
    tokens, channels = x.shape
    positions = WIN * WIN
    windows = tokens // positions
    scale = 1.0 / math.sqrt(channels // heads)
    projected = dot(layer_norm(x, gains[0:1]), entry[...]).astype(bf16)
    for w in range(windows):
        span = slice(w * positions, (w + 1) * positions)
        key = projected[span, channels : 2 * channels]
        spread = jnp.concatenate([key] * heads, axis=0) * mask[...]
        scores = dot_t(projected[span, :channels], spread) * scale + offsets[...]
        exps[span, :] = jnp.exp(scores).astype(bf16)
    for w in range(windows):
        span = slice(w * positions, (w + 1) * positions)
        value = projected[span, 2 * channels :]
        spread = jnp.concatenate([value] * heads, axis=0) * mask[...]
        e = exps[span, :]
        total = dot(e, ones[...])
        weights = (e.astype(f32) / total).astype(bf16)
        mixed[span, :] = dot(weights, spread).astype(bf16)
    attended = (x + dot(mixed[...], leave[...])).astype(bf16).astype(f32)
    second = layer_norm(attended, gains[1:2])
    result = attended
    width = widen.shape[1]
    for part in range(0, width, 256):
        hidden = gelu(dot(second, widen[:, part : part + 256])).astype(bf16)
        result = result + dot(hidden, shrink[part : part + 256, :])
    return result


def kernel(
    dims, xpad, side, cscale, cshift, ew, eb, dk, db, pw,
    bg, be, bl, bo, bw, bs, gg, ge, gl, go, gw, gs, mask, ones, perm, unperm,
    out, ex, side_ex, side_sum, act, exps, mixed, snd, rcv, bsnd,
    send_sem, recv_sem, bsend_sem, brecv_sem,
):
    heads, rp, cp, rg, cg, hc = dims
    group = rg * cg
    rows_here = xpad.shape[0] - 2
    cols_here, channels = xpad.shape[1:]
    inner = ew.shape[1]
    strips = rows_here // WIN
    r, c = lax.axis_index("row"), lax.axis_index("col")
    n_row, n_col = lax.axis_size("row"), lax.axis_size("col")
    me = (r // rp) * cg + c // cp

    def device(slot):
        return ((slot // cg) * rp + lax.rem(r, rp), lax.rem(slot, cg) * cp + lax.rem(c, cp))

    barrier = pltpu.get_barrier_semaphore()

    def greet(d, carry):
        pl.semaphore_signal(
            barrier, inc=1, device_id=device(lax.rem(me + d, group)), device_id_type=MESH
        )
        return carry

    lax.fori_loop(1, group, greet, 0)

    top = (r > 0).astype(f32)
    bottom = (r < n_row - 1).astype(f32)
    left = (c > 0).astype(f32)
    right = (c < n_col - 1).astype(f32)

    def expand(cells, part):
        normed = (cells.astype(f32) * cscale[...] + cshift[...]).astype(bf16)
        lanes = slice(part, part + 256)
        return gelu(dot(normed, ew[:, lanes]) + eb[:, lanes])

    for which in range(2):
        depth = side.shape[1]
        at = lax.broadcasted_iota(jnp.int32, (depth, 256), 0)
        keep = jnp.where(at == 0, top, jnp.where(at == rows_here + 1, bottom, 1.0))
        keep = keep * (left if which == 0 else right)
        for part in range(0, inner, 256):
            side_ex[:, part : part + 256] = expand(side[which], part) * keep
        tap = 0 if which == 0 else 2
        total = side_ex[0:rows_here, :] * dk[tap : tap + 1, :]
        for s in range(1, 3):
            total = total + side_ex[s : s + rows_here, :] * dk[3 * s + tap : 3 * s + tap + 1, :]
        side_sum[which] = total
    for part in range(0, inner, 256):
        first = expand(xpad[0:2].reshape(2 * cols_here, channels), part)
        ex[0:2, :, part : part + 256] = first.reshape(2, cols_here, 256)
    ex[0] = ex[0] * top

    pl.semaphore_wait(barrier, group - 1)

    def send_all(source, target, index, sem_out, sem_in):
        def one(d, carry):
            slot = lax.rem(me + d, group)
            pltpu.make_async_remote_copy(
                src_ref=source.at[index, slot],
                dst_ref=target.at[index, me],
                send_sem=sem_out.at[index],
                recv_sem=sem_in.at[index],
                device_id=device(slot),
                device_id_type=MESH,
            ).start()
            return carry

        lax.fori_loop(1, group, one, 0)

    def await_bytes(ref, index, count, sem):
        part = ref.at[index, pl.ds(0, count)]
        pltpu.make_async_copy(part, part, sem.at[index]).wait()

    def block_strip(i):
        base = i * WIN
        cells = xpad[pl.ds(base + 2, WIN)].reshape(WIN * cols_here, channels)
        for part in range(0, inner, 256):
            grown = expand(cells, part).reshape(WIN, cols_here, 256)
            ex[pl.ds(base + 2, WIN), :, part : part + 256] = grown

        @pl.when(i == strips - 1)
        def _():
            ex[rows_here + 1] = ex[rows_here + 1] * bottom

        near = pl.ds(pl.multiple_of(base, WIN), WIN)

        def chunk(j, carry):
            lanes = pl.ds(pl.multiple_of(j * LANES, LANES), LANES)
            col = lax.broadcasted_iota(jnp.int32, (cols_here, LANES), 0)
            taps = [dk[n : n + 1, lanes] for n in range(9)]
            bias = db[:, lanes]
            lsum = side_sum[0, near, lanes]
            rsum = side_sum[1, near, lanes]
            rows = [ex[base + n, :, lanes] for n in range(WIN + 2)]
            for y in range(WIN):
                a = [
                    taps[t] * rows[y] + taps[3 + t] * rows[y + 1] + taps[6 + t] * rows[y + 2]
                    for t in range(3)
                ]
                low = jnp.where(col == 0, lsum[y : y + 1], pltpu.roll(a[0], 1, 0))
                high = jnp.where(
                    col == cols_here - 1, rsum[y : y + 1], pltpu.roll(a[2], cols_here - 1, 0)
                )
                act[y * cols_here : (y + 1) * cols_here, lanes] = gelu(
                    low + a[1] + high + bias
                ).astype(bf16)
            return carry

        lax.fori_loop(0, inner // LANES, chunk, 0)
        source = xpad[pl.ds(base + 1, WIN)].reshape(WIN * cols_here, channels)
        one = source.astype(f32) + dot(act[...], pw[...])
        one = one.reshape(WIN, cols_here // WIN, WIN, channels).transpose(1, 0, 2, 3)
        one = one.reshape(-1, channels).astype(bf16).astype(f32)
        two = attend(one, heads, bg, be, bl, bo, bw, bs, mask, ones, exps, mixed)
        two = two.reshape(hc, cg, rg, WIN, channels).transpose(2, 1, 0, 3, 4)
        snd[i] = two.reshape(group, hc * WIN, channels).astype(bf16)
        send_all(snd, rcv, i, send_sem, recv_sem)
        rcv[i, me] = snd[i, me]

    def grid_strip(i):
        await_bytes(rcv, i, group - 1, recv_sem)
        tokens = rcv[i].reshape(group * hc * WIN, channels)
        tokens = dot(perm[...], tokens)
        done = attend(tokens, heads, gg, ge, gl, go, gw, gs, mask, ones, exps, mixed)
        done = dot(unperm[...], done.astype(bf16))
        bsnd[i] = done.reshape(group, hc * WIN, channels).astype(bf16)
        send_all(bsnd, out, i, bsend_sem, brecv_sem)
        pltpu.make_async_copy(bsnd.at[i, me], out.at[i, me], brecv_sem.at[i]).start()

    def step(i, carry):
        @pl.when(i < strips)
        def _():
            block_strip(i)

        @pl.when(i >= LAG)
        def _():
            grid_strip(i - LAG)

        return carry

    lax.fori_loop(0, strips + LAG, step, 0)

    def finish(i, carry):
        await_bytes(snd, i, group - 1, send_sem)
        await_bytes(bsnd, i, group - 1, bsend_sem)
        await_bytes(out, i, group, brecv_sem)
        return carry

    lax.fori_loop(0, strips, finish, 0)


def halo(tile):
    def shifted(piece, axis, up):
        count = lax.axis_size(axis)
        pairs = [(i, i + 1) if up else (i + 1, i) for i in range(count - 1)]
        return lax.ppermute(piece, axis, pairs)

    above = shifted(tile[-1:], "row", True)
    below = shifted(tile[:1], "row", False)
    first = jnp.concatenate([above[:, 0], tile[:, 0], below[:, 0]], axis=0)
    last = jnp.concatenate([above[:, -1], tile[:, -1], below[:, -1]], axis=0)
    before = shifted(last, "col", True)
    after = shifted(first, "col", False)
    return jnp.concatenate([above, tile, below], axis=0), jnp.stack([before, after])


def shards(
    radar_tiles, conv_scale, conv_shift, expand_weight, expand_bias, depth_kernel, depth_bias,
    project_weight, block_gains, block_entry, block_leave, block_offsets, block_widen,
    block_shrink, grid_gains, grid_entry, grid_leave, grid_offsets, grid_widen, grid_shrink,
):
    rows_here, cols_here, channels = radar_tiles.shape
    inner = expand_weight.shape[1]
    heads = block_offsets.shape[0]
    n_row, n_col = lax.axis_size("row"), lax.axis_size("col")
    rp, cp = max(1, n_row // WIN), max(1, n_col // WIN)
    rg, cg = min(n_row, WIN), min(n_col, WIN)
    hc = WIN // cg
    group = rg * cg
    strips = rows_here // WIN
    positions = WIN * WIN
    tokens = WIN * cols_here
    xpad, side = halo(radar_tiles)
    side = jnp.pad(side, ((0, 0), (0, -side.shape[1] % 16), (0, 0)))

    def laid(offsets):
        return offsets.transpose(1, 0, 2).reshape(positions, heads * positions)

    at = jnp.arange(heads * positions)
    mask = (at[:, None] // positions == jnp.arange(channels)[None] // (channels // heads)).astype(bf16)
    ones = (at[:, None] // positions == at[None] // positions).astype(bf16)
    order = jnp.arange(tokens)
    source = (order % positions) * WIN + order // positions
    perm = (source[:, None] == order[None]).astype(bf16)
    unperm = (source[None] == order[:, None]).astype(bf16)
    chunk = (strips, group, hc * WIN, channels)
    vmem = pl.BlockSpec(memory_space=pltpu.VMEM)
    operands = (
        xpad, side, conv_scale[None], conv_shift[None], expand_weight, expand_bias[None],
        depth_kernel.reshape(9, inner), depth_bias[None], project_weight,
        block_gains, block_entry, block_leave, laid(block_offsets), block_widen, block_shrink,
        grid_gains, grid_entry, grid_leave, laid(grid_offsets), grid_widen, grid_shrink,
        mask, ones, perm, unperm,
    )
    returned = pl.pallas_call(
        functools.partial(kernel, (heads, rp, cp, rg, cg, hc)),
        out_shape=jax.ShapeDtypeStruct(chunk, bf16),
        in_specs=[vmem] * len(operands),
        out_specs=pl.BlockSpec(memory_space=pl.ANY),
        scratch_shapes=[
            pltpu.VMEM((rows_here + 2, cols_here, inner), f32),
            pltpu.VMEM((side.shape[1], inner), f32),
            pltpu.VMEM((2, rows_here, inner), f32),
            pltpu.VMEM((tokens, inner), bf16),
            pltpu.VMEM((tokens, heads * positions), bf16),
            pltpu.VMEM((tokens, channels), bf16),
            pltpu.VMEM(chunk, bf16),
            pltpu.VMEM(chunk, bf16),
            pltpu.VMEM(chunk, bf16),
            pltpu.SemaphoreType.DMA((strips,)),
            pltpu.SemaphoreType.DMA((strips,)),
            pltpu.SemaphoreType.DMA((strips,)),
            pltpu.SemaphoreType.DMA((strips,)),
        ],
        compiler_params=pltpu.CompilerParams(
            collective_id=0, has_side_effects=True, vmem_limit_bytes=58 * 2**20
        ),
    )(*operands)
    returned = returned.reshape(strips, rg, cg, hc, WIN, channels).transpose(0, 1, 3, 2, 4, 5)
    return returned.reshape(rows_here, cols_here, channels)


def solution(mesh):
    return jax.shard_map(
        shards,
        mesh=mesh,
        in_specs=(P("row", "col", None),) + (P(),) * 19,
        out_specs=P("row", "col", None),
        check_vma=False,
    )
```
